32 devices in a mesh: ctx: 8 (over y, x, core), tp: 4 (over z).
Axes of the slice: x: 2, y: 2, z: 4, core: 2. Of those that a mesh axis runs over, the one named last changes fastest.
Arguments:
- queries: bfloat16 [2048, 8192], P('ctx', 'tp'), may hold values from -22 to 22
- keys: bfloat16 [2048, 512], P('ctx'), may hold values from -22 to 22
- values: bfloat16 [2048, 512], P('ctx'), may hold values from -6 to 6
- grad_out: bfloat16 [2048, 8192], P('ctx', 'tp'), may hold values from -6 to 6
- doc_lengths: int32 [4], replicated, may hold values from 1 to 1024, 2048 in all
Outputs:
- grad_queries: bfloat16 [2048, 8192], P('ctx', 'tp')
- keys_gradient: bfloat16 [2048, 512], P(('ctx', 'tp'))
- values_gradient: bfloat16 [2048, 512], P(('ctx', 'tp'))
The draws below stay inside these ranges and needn't reach their ends.
Inputs may be any that keep to these rules, and one draw needn't show every extreme that they name: `doc_lengths`: they sum to 2048; the longest is exactly 1024.
All inputs are finite; a program needn't handle non-finite values.
Results may differ from the reference program's by a relative error of at most 0.012.
The reference program's roundings to bfloat16 on the way count: a program that leaves them out, or rounds other values in their place, can miss the bound.
Values may be sent and summed in bfloat16 or wider, within the bound.
A program may use at most 192 MiB of HBM per device.

```python
import math
import jax
import jax.numpy as jnp
import numpy as np
from jax import lax

HQ = 64
KV_HEAD_COUNT = 4
HEAD_SIZE = 128
TOK_DEV = 256
MAXDOC = 1024
QUERY_PER_KV = 16
PACK_TOKENS = 2048
DOCS = 4


def draw_keys(key, part):
    key = jax.random.fold_in(key, 3)
    local_part = jnp.clip(jax.random.normal(key, (PACK_TOKENS, KV_HEAD_COUNT, HEAD_SIZE), jnp.float32), -4.0, 4.0)
    return local_part.reshape(PACK_TOKENS, KV_HEAD_COUNT * HEAD_SIZE).astype(jnp.bfloat16)


def draw_queries(key, part):
    key = jax.random.fold_in(key, 5)
    local_part = jnp.clip(jax.random.normal(key, (PACK_TOKENS, KV_HEAD_COUNT, QUERY_PER_KV, HEAD_SIZE), jnp.float32), -4.0, 4.0)
    return local_part.reshape(PACK_TOKENS, HQ * HEAD_SIZE).astype(jnp.bfloat16)


def levels(own_key, shape, shards, least, largest):
    level = 1.0
    for axis_at, shards_of in shards:
        steps = jax.random.uniform(jax.random.fold_in(jax.random.fold_in(own_key, 6), axis_at), (shards_of,), jnp.float32, least / len(shards), largest / len(shards))
        level = level * jnp.repeat(jnp.exp(steps), shape[axis_at] // shards_of).reshape((-1,) + (1,) * (len(shape) - 1 - axis_at))
    return level


def split_up(amount, total, most, slope):
    portions = [(1 << 20) // math.isqrt(rank ** slope) + 1 for rank in range(2, amount + 1)]
    rest, given = total - most - (amount - 1), [1] * (amount - 1)
    while rest > 0:
        movable = [i for i in range(amount - 1) if given[i] < most]
        pool, left = sum([portions[i] for i in movable]), rest
        for i in movable:
            more = min(most - given[i], max(1, left * portions[i] // pool), rest)
            given[i] = given[i] + more
            rest = rest - more
    return np.array([most] + given)


def ragged_sizes(key, number_of, total, bound, skew):
    if number_of == 2:
        one = jax.random.randint(key, (), max(1, total - bound), min(bound, total - 1) + 1)
        return jnp.stack([one, total - one])
    sizes = jnp.asarray(split_up(number_of, total, bound, skew), jnp.int32)
    twos = (number_of - 1) // 2
    donor, taker = sizes[1:1 + 2 * twos:2], sizes[2:2 + 2 * twos:2]
    margin = jnp.minimum(donor - 1, bound - taker)
    moved = jax.random.randint(jax.random.fold_in(key, 1), (twos,), 0, 1 << 20) % (margin + 1)
    sizes = sizes.at[1:1 + 2 * twos:2].set(donor - moved).at[2:2 + 2 * twos:2].set(taker + moved)
    return sizes[jax.random.permutation(jax.random.fold_in(key, 2), number_of)]


def noise(stream_key, shape, spread, limit, cuts=(), kind=jnp.bfloat16):
    drawn = spread * jax.random.normal(stream_key, shape, jnp.float32)
    if cuts:
        drawn = drawn * levels(stream_key, shape, cuts, -0.22, 0.18)
    return jnp.clip(drawn, -limit, limit).astype(kind)


def setup_inputs(seed: int = 0) -> dict:
    key_of = jax.random.split(jax.random.key(seed), 6)
    queries = draw_queries(jax.random.fold_in(key_of[5], 71), 0)
    keys = draw_keys(jax.random.fold_in(key_of[5], 71), 0)
    values = noise(key_of[2], (PACK_TOKENS, KV_HEAD_COUNT * HEAD_SIZE), 1.0, 6.0, ((0, 8),))
    grad_out = noise(key_of[3], (PACK_TOKENS, HQ * HEAD_SIZE), 1.0, 6.0, ((0, 8), (1, 4)))
    doc_lengths = ragged_sizes(key_of[4], DOCS, PACK_TOKENS, MAXDOC, 2).astype(jnp.int32)
    return {"queries": queries, "keys": keys, "values": values, "grad_out": grad_out, "doc_lengths": doc_lengths}


NEG = -1.0e30


def doc_pos(doc_lengths, first, item_count):
    starts = (jnp.cumsum(doc_lengths) - doc_lengths).astype(jnp.int32)
    tok = (first + jnp.arange(item_count, dtype=jnp.int32)).astype(jnp.int32)
    before = starts[None, :] <= tok[:, None]
    docid = (jnp.sum(before.astype(jnp.int32), axis=1) - 1).astype(jnp.int32)
    onehot = docid[:, None] == jnp.arange(starts.shape[0], dtype=jnp.int32)[None, :]
    start_of = jnp.sum(jnp.where(onehot, starts[None, :], 0), axis=1).astype(jnp.int32)
    return tok, docid, (tok - start_of).astype(jnp.int32)


def rope_tables(pos):
    half = HEAD_SIZE // 2
    freq = 500000.0 ** (-(2.0 * jnp.arange(half, dtype=jnp.float32)) / HEAD_SIZE)
    angle = pos.astype(jnp.float32)[:, None] * freq[None, :]
    return jnp.cos(angle), jnp.sin(angle)


def apply_rotary(x, cosine_table, sine_table):
    half = HEAD_SIZE // 2
    first, second = x[..., :half], x[..., half:]
    c, s = cosine_table[:, None, :], sine_table[:, None, :]
    return jnp.concatenate([first * c - second * s, second * c + first * s], axis=-1)


def invert_rotary(y, cosine_table, sine_table):
    half = HEAD_SIZE // 2
    first, second = y[..., :half], y[..., half:]
    c, s = cosine_table[:, None, :], sine_table[:, None, :]
    return jnp.concatenate([first * c + second * s, second * c - first * s], axis=-1)


def reference(queries, keys, values, grad_out, doc_lengths):
    tok, docid, pos = doc_pos(doc_lengths, 0, PACK_TOKENS)
    cosine_table, sine_table = rope_tables(pos)
    rot_q = apply_rotary(queries.reshape(PACK_TOKENS, HQ, HEAD_SIZE).astype(jnp.float32), cosine_table, sine_table).astype(jnp.bfloat16)
    rotated_keys = apply_rotary(keys.reshape(PACK_TOKENS, KV_HEAD_COUNT, HEAD_SIZE).astype(jnp.float32), cosine_table, sine_table).astype(jnp.bfloat16)
    value_rows = values.reshape(PACK_TOKENS, KV_HEAD_COUNT, HEAD_SIZE)
    grads = grad_out.reshape(PACK_TOKENS, HQ, HEAD_SIZE)
    width = min(PACK_TOKENS, TOK_DEV + MAXDOC)
    scale = HEAD_SIZE ** -0.5

    def single_head(head):
        q_head = lax.dynamic_slice_in_dim(rot_q, head * QUERY_PER_KV, QUERY_PER_KV, 1).astype(jnp.float32)
        g_head = lax.dynamic_slice_in_dim(grads, head * QUERY_PER_KV, QUERY_PER_KV, 1).astype(jnp.float32)
        k_head = lax.dynamic_index_in_dim(rotated_keys, head, 1, keepdims=False).astype(jnp.float32)
        v_head = lax.dynamic_index_in_dim(value_rows, head, 1, keepdims=False).astype(jnp.float32)

        def block(carry, index):
            dk_acc, dv_acc = carry
            first = (index * TOK_DEV).astype(jnp.int32)
            low = jnp.maximum(first + TOK_DEV - width, 0).astype(jnp.int32)
            q_blk = lax.dynamic_slice_in_dim(q_head, first, TOK_DEV, 0)
            g_blk = lax.dynamic_slice_in_dim(g_head, first, TOK_DEV, 0)
            k_blk = lax.dynamic_slice_in_dim(k_head, low, width, 0)
            v_blk = lax.dynamic_slice_in_dim(v_head, low, width, 0)
            q_tok = lax.dynamic_slice_in_dim(tok, first, TOK_DEV, 0)
            q_doc = lax.dynamic_slice_in_dim(docid, first, TOK_DEV, 0)
            k_tok = lax.dynamic_slice_in_dim(tok, low, width, 0)
            k_doc = lax.dynamic_slice_in_dim(docid, low, width, 0)
            allowed = (q_doc[:, None] == k_doc[None, :]) & (k_tok[None, :] <= q_tok[:, None])
            score = jnp.einsum('qgd,kd->gqk', q_blk, k_blk) * scale
            score = jnp.where(allowed[None], score, NEG)
            top = jnp.max(score, axis=2, keepdims=True)
            lse = top + jnp.log(jnp.sum(jnp.exp(score - top), axis=2, keepdims=True))
            prob = jnp.exp(score - lse)
            dprod = jnp.einsum('qgd,kd->gqk', g_blk, v_blk)
            delta = jnp.sum(prob * dprod, axis=2, keepdims=True)
            prob_b = lax.optimization_barrier(prob.astype(jnp.bfloat16)).astype(jnp.float32)
            dv_blk = jnp.einsum('gqk,qgd->kd', prob_b, g_blk)
            dscore = (prob * (dprod - delta) * scale).astype(jnp.bfloat16)
            dscore = lax.optimization_barrier(dscore).astype(jnp.float32)
            dq_blk = jnp.einsum('gqk,kd->qgd', dscore, k_blk)
            dk_blk = jnp.einsum('gqk,qgd->kd', dscore, q_blk)
            dk_acc = lax.dynamic_update_slice_in_dim(dk_acc, lax.dynamic_slice_in_dim(dk_acc, low, width, 0) + dk_blk, low, 0)
            dv_acc = lax.dynamic_update_slice_in_dim(dv_acc, lax.dynamic_slice_in_dim(dv_acc, low, width, 0) + dv_blk, low, 0)
            return (dk_acc, dv_acc), dq_blk

        zero_block = jnp.zeros((PACK_TOKENS, HEAD_SIZE), jnp.float32)
        (dk_acc, dv_acc), dq_blocks = lax.scan(block, (zero_block, zero_block), jnp.arange(PACK_TOKENS // TOK_DEV, dtype=jnp.int32))
        return dq_blocks.reshape(PACK_TOKENS, QUERY_PER_KV, HEAD_SIZE), dk_acc, dv_acc

    query_grad_total, key_grad_total, value_grad_total = lax.map(single_head, jnp.arange(KV_HEAD_COUNT, dtype=jnp.int32))
    query_grad_total = jnp.transpose(query_grad_total, (1, 0, 2, 3)).reshape(PACK_TOKENS, HQ, HEAD_SIZE)
    grad_queries = invert_rotary(query_grad_total, cosine_table, sine_table).astype(jnp.bfloat16).reshape(PACK_TOKENS, HQ * HEAD_SIZE)
    key_grad_total = jnp.transpose(key_grad_total, (1, 0, 2))
    keys_gradient = invert_rotary(key_grad_total, cosine_table, sine_table).astype(jnp.bfloat16).reshape(PACK_TOKENS, KV_HEAD_COUNT * HEAD_SIZE)
    values_gradient = jnp.transpose(value_grad_total, (1, 0, 2)).astype(jnp.bfloat16).reshape(PACK_TOKENS, KV_HEAD_COUNT * HEAD_SIZE)
    return (grad_queries, keys_gradient, values_gradient)
```

```python
import functools
import math

import jax
import jax.numpy as jnp
from jax import lax
from jax.experimental import pallas as pl
from jax.experimental.pallas import tpu as pltpu
from jax.sharding import PartitionSpec as P

KV_HEAD_COUNT = 4
HEAD_SIZE = 128
QUERY_PER_KV = 16
MAXDOC = 1024
NEG = -1e30
HALF = HEAD_SIZE // 2
SCALE = HEAD_SIZE ** (-0.5)
LOG2E = math.log2(math.e)
HEADS_PER_STEP = 2
VMEM_LIMIT = 48 << 20
MESH = pl.DeviceIdType.MESH


def doc_pos(doc_lengths, first, item_count):
    starts = jnp.cumsum(doc_lengths) - doc_lengths
    tok = first + jnp.arange(item_count, dtype=jnp.int32)
    start_of = jnp.max(jnp.where(starts[None, :] <= tok[:, None], starts[None, :], 0), axis=1)
    return tok, start_of, tok - start_of


def rope_tables(pos):
    freq = 500000.0 ** (-(2.0 * jnp.arange(HALF, dtype=jnp.float32)) / HEAD_SIZE)
    angle = pos.astype(jnp.float32)[:, None] * freq[None, :]
    return jnp.cos(angle), jnp.sin(angle)


def greet(peers):
    barrier = pltpu.get_barrier_semaphore()
    count = 0
    for live, device in peers:
        @pl.when(live)
        def _():
            pl.semaphore_signal(barrier, inc=1, device_id=device, device_id_type=MESH)
        count = count + live.astype(jnp.int32)
    pl.semaphore_wait(barrier, count)


def gather_kernel(n_ctx, reach, own_ref, win_ref, send_sem, recv_sem, local_sem):
    rows = own_ref.shape[1]
    me = lax.axis_index("ctx")
    at = lax.axis_index("tp")
    greet(
        [(me + s < n_ctx, (lax.rem(me + s, n_ctx), at)) for s in range(1, reach + 1)]
        + [(me - s >= 0, (lax.rem(me - s + n_ctx, n_ctx), at)) for s in range(1, reach + 1)]
    )

    def copy(s):
        return pltpu.make_async_remote_copy(
            src_ref=own_ref,
            dst_ref=win_ref.at[:, pl.ds((reach - s) * rows, rows), :],
            send_sem=send_sem.at[s - 1],
            recv_sem=recv_sem.at[s - 1],
            device_id=(lax.rem(me + s, n_ctx), at),
            device_id_type=MESH,
        )

    for s in range(reach, 0, -1):
        @pl.when(me + s < n_ctx)
        def _():
            copy(s).start()
    mine = pltpu.make_async_copy(own_ref, win_ref.at[:, pl.ds(reach * rows, rows), :], local_sem)
    mine.start()
    mine.wait()
    for s in range(1, reach + 1):
        @pl.when(me - s >= 0)
        def _():
            copy(s).wait_recv()
    for s in range(1, reach + 1):
        @pl.when(me + s < n_ctx)
        def _():
            copy(s).wait_send()


def gather(own, n_ctx, reach):
    two, rows, width = own.shape
    return pl.pallas_call(
        functools.partial(gather_kernel, n_ctx, reach),
        out_shape=jax.ShapeDtypeStruct((two, (reach + 1) * rows, width), own.dtype),
        in_specs=[pl.BlockSpec(memory_space=pl.ANY)],
        out_specs=pl.BlockSpec(memory_space=pl.ANY),
        scratch_shapes=[
            pltpu.SemaphoreType.DMA((reach,)),
            pltpu.SemaphoreType.DMA((reach,)),
            pltpu.SemaphoreType.DMA,
        ],
        compiler_params=pltpu.CompilerParams(collective_id=0, has_side_effects=True),
        name="gather_kv",
    )(own)


def attend_kernel(
    reach, rows, low_ref, win_ref, q_ref, g_ref, cos_ref, sin_ref, cos_t_ref, sin_t_ref, start_ref,
    dq_ref, far_ref, own_ref, bias, kt, dk, dv,
):
    step = pl.program_id(0)
    span = (reach + 1) * rows

    @pl.when(step == 0)
    def _():
        key = lax.broadcasted_iota(jnp.int32, (span, rows), 0)
        query = lax.broadcasted_iota(jnp.int32, (span, rows), 1) + reach * rows
        allowed = (key >= start_ref[...]) & (key <= query)
        bias[...] = jnp.where(allowed, 0.0, NEG)
        kt[...] = win_ref[0].T
        dk[...] = jnp.zeros_like(dk)
        dv[...] = jnp.zeros_like(dv)

    nt = (((1,), (1,)), ((), ()))

    def work(tiles):
        base = span - tiles * rows
        keys = win_ref[0, base:, :]
        values = win_ref[1, base:, :]
        probs, grads, dscores, queries = [], [], [], []
        for i in range(HEADS_PER_STEP):
            cols = slice(i * HEAD_SIZE, (i + 1) * HEAD_SIZE)
            raw = q_ref[:, cols].astype(jnp.float32)
            rot = raw * cos_ref[...] + pltpu.roll(raw, HALF, 1) * sin_ref[...]
            rot = rot.astype(jnp.bfloat16)
            grad = g_ref[:, cols]
            score = lax.dot_general(keys, rot, nt, preferred_element_type=jnp.float32)
            score = score * (SCALE * LOG2E) + bias[base:, :]
            top = jnp.max(score, axis=0, keepdims=True)
            expo = jnp.exp2(score - top)
            total = jnp.sum(expo, axis=0, keepdims=True)
            dprod = lax.dot_general(values, grad, nt, preferred_element_type=jnp.float32)
            weighted = jnp.sum(expo * dprod, axis=0, keepdims=True)
            inv = 1.0 / total
            delta = weighted * inv
            probs.append(expo.astype(jnp.bfloat16))
            dscore = (expo * (dprod - delta)).astype(jnp.bfloat16)
            dscores.append(dscore)
            spread = jnp.broadcast_to(inv, (HEAD_SIZE, rows)).T
            grads.append((grad.astype(jnp.float32) * spread).astype(jnp.bfloat16))
            queries.append((rot.astype(jnp.float32) * (spread * SCALE)).astype(jnp.bfloat16))
            dq = jnp.dot(kt[:, base:], dscore, preferred_element_type=jnp.float32)
            dq = dq * (inv * SCALE)
            one, two = dq[:HALF], dq[HALF:]
            c, s = cos_t_ref[...], sin_t_ref[...]
            turned = jnp.concatenate([one * c + two * s, two * c - one * s], axis=0)
            dq_ref[:, cols] = turned.T.astype(jnp.bfloat16)
        dv[base:, :] += jnp.dot(
            jnp.concatenate(probs, axis=1), jnp.concatenate(grads, axis=0),
            preferred_element_type=jnp.float32,
        )
        dk[base:, :] += jnp.dot(
            jnp.concatenate(dscores, axis=1), jnp.concatenate(queries, axis=0),
            preferred_element_type=jnp.float32,
        )

    tiles = reach + 1 - low_ref[0] // rows
    for count in range(1, reach + 2):
        @pl.when(tiles == count)
        def _():
            work(count)

    @pl.when(step == pl.num_programs(0) - 1)
    def _():
        far_ref[0] = dk[: reach * rows, :].astype(jnp.bfloat16)
        far_ref[1] = dv[: reach * rows, :].astype(jnp.bfloat16)
        own_ref[0] = dk[reach * rows :, :]
        own_ref[1] = dv[reach * rows :, :]


def attend(window, queries, grad_out, low, start_row, cos, sin, reach):
    rows, width = queries.shape
    span = (reach + 1) * rows
    block = HEADS_PER_STEP * HEAD_SIZE
    steps = width // block
    cos_wide = jnp.concatenate([cos, cos], axis=1)
    sin_wide = jnp.concatenate([-sin, sin], axis=1)

    def whole(shape):
        return pl.BlockSpec(shape, lambda i, low: (0,) * len(shape))

    by_head = pl.BlockSpec((rows, block), lambda i, low: (0, i))
    return pl.pallas_call(
        functools.partial(attend_kernel, reach, rows),
        grid_spec=pltpu.PrefetchScalarGridSpec(
            num_scalar_prefetch=1,
            grid=(steps,),
            in_specs=[
                whole((2, span, HEAD_SIZE)), by_head, by_head,
                whole((rows, HEAD_SIZE)), whole((rows, HEAD_SIZE)),
                whole((HALF, rows)), whole((HALF, rows)), whole((1, rows)),
            ],
            out_specs=[
                by_head, whole((2, reach * rows, HEAD_SIZE)), whole((2, rows, HEAD_SIZE)),
            ],
            scratch_shapes=[
                pltpu.VMEM((span, rows), jnp.float32),
                pltpu.VMEM((HEAD_SIZE, span), jnp.bfloat16),
                pltpu.VMEM((span, HEAD_SIZE), jnp.float32),
                pltpu.VMEM((span, HEAD_SIZE), jnp.float32),
            ],
        ),
        out_shape=[
            jax.ShapeDtypeStruct((rows, width), jnp.bfloat16),
            jax.ShapeDtypeStruct((2, reach * rows, HEAD_SIZE), jnp.bfloat16),
            jax.ShapeDtypeStruct((2, rows, HEAD_SIZE), jnp.float32),
        ],
        compiler_params=pltpu.CompilerParams(
            dimension_semantics=("arbitrary",), vmem_limit_bytes=VMEM_LIMIT
        ),
        name="attend",
    )(low, window, queries, grad_out, cos_wide, sin_wide, cos.T, sin.T, start_row)


def scatter_kernel(
    n_ctx, n_tp, reach, share, far_ref, own_ref, cos_ref, sin_ref, key_out, value_out,
    acc, landed, staged, pieces, send_sem, recv_sem, piece_send, piece_recv,
):
    rows = own_ref.shape[1]
    items = rows // n_tp
    me = lax.axis_index("ctx")
    at = lax.axis_index("tp")
    greet(
        [(me - s >= 0, (lax.rem(me - s + n_ctx, n_ctx), at)) for s in range(1, reach + 1)]
        + [(me + s < n_ctx, (lax.rem(me + s, n_ctx), at)) for s in range(1, reach + 1)]
        + [(at >= 0, (me, lax.rem(at + t, n_tp))) for t in range(1, n_tp)]
    )

    def copy(s):
        return pltpu.make_async_remote_copy(
            src_ref=far_ref.at[:, pl.ds((reach - s) * rows, rows), :],
            dst_ref=landed.at[s - 1],
            send_sem=send_sem.at[s - 1],
            recv_sem=recv_sem.at[s - 1],
            device_id=(lax.rem(me - s + n_ctx, n_ctx), at),
            device_id_type=MESH,
        )

    for s in range(reach, 0, -1):
        @pl.when(me - s >= 0)
        def _():
            copy(s).start()
    acc[...] = own_ref[...]
    for s in range(1, reach + 1):
        @pl.when(me + s < n_ctx)
        def _():
            copy(s).wait_recv()
            acc[...] += landed[s - 1].astype(jnp.float32)
    grad = acc[0]
    turned = grad * cos_ref[...] - pltpu.roll(grad, HALF, 1) * sin_ref[...]
    staged[0] = turned.astype(staged.dtype)
    staged[1] = acc[1].astype(staged.dtype)

    def piece(t):
        to = lax.rem(at + t, n_tp)
        return pltpu.make_async_remote_copy(
            src_ref=staged.at[:, pl.ds(pl.multiple_of(to * items, items), items), :],
            dst_ref=pieces.at[t],
            send_sem=piece_send.at[t - 1],
            recv_sem=piece_recv.at[t - 1],
            device_id=(me, to),
            device_id_type=MESH,
        )

    for t in range(1, n_tp):
        piece(t).start()
    pieces[0] = staged[:, pl.ds(pl.multiple_of(at * items, items), items), :]
    for t in range(1, n_tp):
        piece(t).wait_recv()
    for head in range(KV_HEAD_COUNT):
        cols = slice(head * HEAD_SIZE, (head + 1) * HEAD_SIZE)
        total = None
        for other in range(head * share, (head + 1) * share):
            got = pieces[lax.rem(at - other + n_tp, n_tp)]
            total = got if total is None else total + got
        key_out[:, cols] = total[0].astype(jnp.bfloat16)
        value_out[:, cols] = total[1].astype(jnp.bfloat16)
    for t in range(1, n_tp):
        piece(t).wait_send()
    for s in range(1, reach + 1):
        @pl.when(me - s >= 0)
        def _():
            copy(s).wait_send()


def scatter(far, own, cos_wide, sin_wide, n_ctx, n_tp, reach, share):
    rows = own.shape[1]
    items = rows // n_tp
    between = jnp.bfloat16 if share == 1 else jnp.float32
    vmem = pl.BlockSpec(memory_space=pltpu.VMEM)
    width = KV_HEAD_COUNT * HEAD_SIZE
    return pl.pallas_call(
        functools.partial(scatter_kernel, n_ctx, n_tp, reach, share),
        out_shape=[jax.ShapeDtypeStruct((items, width), jnp.bfloat16)] * 2,
        in_specs=[vmem] * 4,
        out_specs=[vmem] * 2,
        scratch_shapes=[
            pltpu.VMEM((2, rows, HEAD_SIZE), jnp.float32),
            pltpu.VMEM((reach, 2, rows, HEAD_SIZE), jnp.bfloat16),
            pltpu.VMEM((2, rows, HEAD_SIZE), between),
            pltpu.VMEM((n_tp, 2, items, HEAD_SIZE), between),
            pltpu.SemaphoreType.DMA((reach,)),
            pltpu.SemaphoreType.DMA((reach,)),
            pltpu.SemaphoreType.DMA((n_tp - 1,)),
            pltpu.SemaphoreType.DMA((n_tp - 1,)),
        ],
        compiler_params=pltpu.CompilerParams(
            collective_id=1, has_side_effects=True, vmem_limit_bytes=VMEM_LIMIT
        ),
        name="scatter_grads",
    )(far, own, cos_wide, sin_wide)


def local(queries, keys, values, grad_out, doc_lengths):
    rows = queries.shape[0]
    heads = queries.shape[1] // HEAD_SIZE
    n_ctx = lax.axis_size("ctx")
    n_tp = lax.axis_size("tp")
    at = lax.axis_index("tp")
    head = at * heads // QUERY_PER_KV
    share = max(1, QUERY_PER_KV // heads)
    reach = min(-(-MAXDOC // rows), n_ctx - 1)
    first = lax.axis_index("ctx") * rows
    tok, start_of, pos = doc_pos(doc_lengths, first, rows)
    cos, sin = rope_tables(pos)
    start_row = (start_of - (first - reach * rows))[None, :]
    low = start_row[0, :1]
    key = lax.dynamic_slice_in_dim(keys, head * HEAD_SIZE, HEAD_SIZE, 1).astype(jnp.float32)
    value = lax.dynamic_slice_in_dim(values, head * HEAD_SIZE, HEAD_SIZE, 1)
    one, two = key[:, :HALF], key[:, HALF:]
    key = jnp.concatenate([one * cos - two * sin, two * cos + one * sin], axis=1)
    own = jnp.stack([key.astype(jnp.bfloat16), value])
    window = gather(own, n_ctx, reach)
    grad_queries, far, near = attend(window, queries, grad_out, low, start_row, cos, sin, reach)
    cos_wide = jnp.concatenate([cos, cos], axis=1)
    sin_wide = jnp.concatenate([-sin, sin], axis=1)
    keys_gradient, values_gradient = scatter(
        far, near, cos_wide, sin_wide, n_ctx, n_tp, reach, share
    )
    return grad_queries, keys_gradient, values_gradient


def solution(mesh):
    return jax.shard_map(
        local,
        mesh=mesh,
        in_specs=(P("ctx", "tp"), P("ctx", None), P("ctx", None), P("ctx", "tp"), P()),
        out_specs=(P("ctx", "tp"), P(("ctx", "tp"), None), P(("ctx", "tp"), None)),
        check_vma=False,
    )
```

```python
import functools
import math

import jax
import jax.numpy as jnp
import numpy as np
from jax import lax
from jax.experimental import pallas as pl
from jax.experimental.pallas import tpu as pltpu
from jax.sharding import PartitionSpec as P

KV_HEAD_COUNT = 4
HEAD_SIZE = 128
QUERY_PER_KV = 16
MAXDOC = 1024
NEG = -1e30
HALF = HEAD_SIZE // 2
SCALE = HEAD_SIZE ** (-0.5)
LOG2E = math.log2(math.e)
HEADS_PER_STEP = 2
VMEM_LIMIT = 48 << 20
MESH = pl.DeviceIdType.MESH


def greet(peers):
    barrier = pltpu.get_barrier_semaphore()
    count = 0
    for live, device in peers:
        @pl.when(live)
        def _():
            pl.semaphore_signal(barrier, inc=1, device_id=device, device_id_type=MESH)
        count = count + live.astype(jnp.int32)
    pl.semaphore_wait(barrier, count)


def doc_starts(lengths_ref, tok):
    start = jnp.int32(0)
    found = jnp.zeros_like(tok)
    for d in range(lengths_ref.shape[0]):
        found = jnp.where(tok >= start, start, found)
        start = start + lengths_ref[d]
    return found


def gather_kernel(
    n_ctx, reach, heads, lengths_ref, freq_ref, keys_ref, values_ref,
    rk_ref, v_ref, kt_ref, cos_ref, sin_ref, cos_t_ref, sin_t_ref,
    raw, cos_all, sin_all, send_sem, recv_sem, local_sem,
):
    rows = keys_ref.shape[0]
    me = lax.axis_index("ctx")
    at = lax.axis_index("tp")
    head = at * heads // QUERY_PER_KV
    cols = pl.ds(pl.multiple_of(head * HEAD_SIZE, HEAD_SIZE), HEAD_SIZE)
    here = pl.ds(reach * rows, rows)
    own_key = pltpu.make_async_copy(keys_ref.at[:, cols], raw.at[0, here, :], local_sem.at[0])
    own_value = pltpu.make_async_copy(values_ref.at[:, cols], raw.at[1, here, :], local_sem.at[1])
    own_key.start()
    own_value.start()
    greet(
        [(me + s < n_ctx, (lax.rem(me + s, n_ctx), at)) for s in range(1, reach + 1)]
        + [(me - s >= 0, (lax.rem(me - s + n_ctx, n_ctx), at)) for s in range(1, reach + 1)]
    )
    own_key.wait()
    own_value.wait()

    def copy(s):
        return pltpu.make_async_remote_copy(
            src_ref=raw.at[:, here, :],
            dst_ref=raw.at[:, pl.ds((reach - s) * rows, rows), :],
            send_sem=send_sem.at[s - 1],
            recv_sem=recv_sem.at[s - 1],
            device_id=(lax.rem(me + s, n_ctx), at),
            device_id_type=MESH,
        )

    for s in range(reach, 0, -1):
        @pl.when(me + s < n_ctx)
        def _():
            copy(s).start()

    freq = freq_ref[:, :1]
    for slot in range(reach, -1, -1):
        lanes = slice(slot * rows, (slot + 1) * rows)
        tok = lax.broadcasted_iota(jnp.int32, (1, rows), 1) + (me - reach + slot) * rows
        pos = (tok - doc_starts(lengths_ref, tok)).astype(jnp.float32)
        angle = pos * freq
        cos_all[:, lanes] = jnp.cos(angle)
        sin_all[:, lanes] = jnp.sin(angle)
    cos = cos_all[:, reach * rows :]
    sin = sin_all[:, reach * rows :]
    cos_t_ref[...] = cos
    sin_t_ref[...] = sin
    cos_ref[...] = jnp.concatenate([cos, cos], axis=0).T
    sin_ref[...] = jnp.concatenate([-sin, sin], axis=0).T

    def turn(slot):
        lanes = slice(slot * rows, (slot + 1) * rows)
        key = raw[0, lanes, :].astype(jnp.float32).T
        one, two = key[:HALF], key[HALF:]
        c, s = cos_all[:, lanes], sin_all[:, lanes]
        key = jnp.concatenate([one * c - two * s, two * c + one * s], axis=0)
        kt_ref[:, lanes] = key.astype(jnp.bfloat16)
        rk_ref[lanes, :] = key.T.astype(jnp.bfloat16)
        v_ref[lanes, :] = raw[1, lanes, :]

    turn(reach)
    for s in range(1, reach + 1):
        @pl.when(me - s >= 0)
        def _():
            copy(s).wait_recv()
            turn(reach - s)
    for s in range(1, reach + 1):
        @pl.when(me + s < n_ctx)
        def _():
            copy(s).wait_send()


def gather(keys, values, doc_lengths, heads, n_ctx, reach):
    rows = keys.shape[0]
    span = (reach + 1) * rows
    freq = np.float32(500000.0) ** (-(2.0 * np.arange(HALF, dtype=np.float32)) / HEAD_SIZE)
    freq = jnp.asarray(np.broadcast_to(freq.astype(np.float32)[:, None], (HALF, HEAD_SIZE)))
    vmem = pl.BlockSpec(memory_space=pltpu.VMEM)
    hbm = pl.BlockSpec(memory_space=pl.ANY)
    return pl.pallas_call(
        functools.partial(gather_kernel, n_ctx, reach, heads),
        out_shape=[
            jax.ShapeDtypeStruct((span, HEAD_SIZE), jnp.bfloat16),
            jax.ShapeDtypeStruct((span, HEAD_SIZE), jnp.bfloat16),
            jax.ShapeDtypeStruct((HEAD_SIZE, span), jnp.bfloat16),
            jax.ShapeDtypeStruct((rows, HEAD_SIZE), jnp.float32),
            jax.ShapeDtypeStruct((rows, HEAD_SIZE), jnp.float32),
            jax.ShapeDtypeStruct((HALF, rows), jnp.float32),
            jax.ShapeDtypeStruct((HALF, rows), jnp.float32),
        ],
        in_specs=[pl.BlockSpec(memory_space=pltpu.SMEM), vmem, hbm, hbm],
        out_specs=[vmem] * 7,
        scratch_shapes=[
            pltpu.VMEM((2, span, HEAD_SIZE), jnp.bfloat16),
            pltpu.VMEM((HALF, span), jnp.float32),
            pltpu.VMEM((HALF, span), jnp.float32),
            pltpu.SemaphoreType.DMA((reach,)),
            pltpu.SemaphoreType.DMA((reach,)),
            pltpu.SemaphoreType.DMA((2,)),
        ],
        compiler_params=pltpu.CompilerParams(
            collective_id=0, has_side_effects=True, vmem_limit_bytes=VMEM_LIMIT
        ),
        name="gather_kv",
    )(doc_lengths, freq, keys, values)


def attend_kernel(
    reach, rows, lengths_ref, rk_ref, v_ref, kt_ref, cos_ref, sin_ref, cos_t_ref, sin_t_ref,
    q_ref, g_ref, dq_ref, far_ref, own_ref, bias, dk, dv, rots,
):
    step = pl.program_id(0)
    span = (reach + 1) * rows
    half = rows // 2
    first = lax.axis_index("ctx") * rows

    @pl.when(step == 0)
    def _():
        query = lax.broadcasted_iota(jnp.int32, (1, rows), 1) + reach * rows
        start = doc_starts(lengths_ref, query + (first - reach * rows)) - (first - reach * rows)
        key = lax.broadcasted_iota(jnp.int32, (span, rows), 0)
        bias[...] = jnp.where((key >= start) & (key <= query), 0.0, NEG)
        dk[...] = jnp.zeros_like(dk)
        dv[...] = jnp.zeros_like(dv)

    nt = (((1,), (1,)), ((), ()))
    for i in range(HEADS_PER_STEP):
        cols = slice(i * HEAD_SIZE, (i + 1) * HEAD_SIZE)
        raw = q_ref[:, cols].astype(jnp.float32)
        rot = raw * cos_ref[...] + pltpu.roll(raw, HALF, 1) * sin_ref[...]
        rots[:, cols] = rot.astype(jnp.bfloat16)

    def pick(ref, side, pair):
        return jnp.concatenate(
            [
                ref[side * half : (side + 1) * half, i * HEAD_SIZE : (i + 1) * HEAD_SIZE]
                for i in (2 * pair, 2 * pair + 1)
            ],
            axis=0,
        )

    def twice(x):
        return jnp.concatenate([x, x], axis=1)

    def work(side, count):
        end = span - half + side * half
        base = end - count * half
        keys = rk_ref[base:end, :]
        values = v_ref[base:end, :]
        lanes = slice(side * half, (side + 1) * half)
        mask = twice(bias[base:end, lanes])
        c, s = twice(cos_t_ref[:, lanes]), twice(sin_t_ref[:, lanes])
        probs, grads, dscores, queries = [], [], [], []
        for pair in range(HEADS_PER_STEP // 2):
            rot = pick(rots, side, pair)
            grad = pick(g_ref, side, pair)
            score = lax.dot_general(keys, rot, nt, preferred_element_type=jnp.float32)
            score = score * (SCALE * LOG2E) + mask
            top = jnp.max(score, axis=0, keepdims=True)
            expo = jnp.exp2(score - top)
            total = jnp.sum(expo, axis=0, keepdims=True)
            dprod = lax.dot_general(values, grad, nt, preferred_element_type=jnp.float32)
            weighted = jnp.sum(expo * dprod, axis=0, keepdims=True)
            inv = 1.0 / total
            delta = weighted * inv
            probs.append(expo.astype(jnp.bfloat16))
            dscore = (expo * (dprod - delta)).astype(jnp.bfloat16)
            dscores.append(dscore)
            spread = jnp.broadcast_to(inv, (HEAD_SIZE, 2 * half)).T
            grads.append((grad.astype(jnp.float32) * spread).astype(jnp.bfloat16))
            queries.append((rot.astype(jnp.float32) * (spread * SCALE)).astype(jnp.bfloat16))
            dq = jnp.dot(kt_ref[:, base:end], dscore, preferred_element_type=jnp.float32)
            dq = dq * (inv * SCALE)
            one, two = dq[:HALF], dq[HALF:]
            turned = jnp.concatenate([one * c + two * s, two * c - one * s], axis=0)
            turned = turned.astype(jnp.bfloat16).T
            for i in range(2):
                at = (2 * pair + i) * HEAD_SIZE
                dq_ref[lanes, at : at + HEAD_SIZE] = turned[i * half : (i + 1) * half, :]
        dv[base:end, :] += jnp.dot(
            jnp.concatenate(probs, axis=1), jnp.concatenate(grads, axis=0),
            preferred_element_type=jnp.float32,
        )
        dk[base:end, :] += jnp.dot(
            jnp.concatenate(dscores, axis=1), jnp.concatenate(queries, axis=0),
            preferred_element_type=jnp.float32,
        )

    for side in range(2):
        tok = first + side * half
        low = doc_starts(lengths_ref, tok) - (first - reach * rows)
        most = 2 * reach + 1 + side
        tiles = most - low // half
        for count in range(1, most + 1):
            @pl.when(tiles == count)
            def _():
                work(side, count)

    @pl.when(step == pl.num_programs(0) - 1)
    def _():
        far_ref[0] = dk[: reach * rows, :].astype(jnp.bfloat16)
        far_ref[1] = dv[: reach * rows, :].astype(jnp.bfloat16)
        own_ref[0] = dk[reach * rows :, :]
        own_ref[1] = dv[reach * rows :, :]


def attend(window, queries, grad_out, doc_lengths, reach):
    rows, width = queries.shape
    span = (reach + 1) * rows
    block = HEADS_PER_STEP * HEAD_SIZE

    def whole(shape):
        return pl.BlockSpec(shape, lambda i, low: (0,) * len(shape))

    by_head = pl.BlockSpec((rows, block), lambda i, low: (0, i))
    return pl.pallas_call(
        functools.partial(attend_kernel, reach, rows),
        grid_spec=pltpu.PrefetchScalarGridSpec(
            num_scalar_prefetch=1,
            grid=(width // block,),
            in_specs=[whole(x.shape) for x in window] + [by_head, by_head],
            out_specs=[
                by_head, whole((2, reach * rows, HEAD_SIZE)), whole((2, rows, HEAD_SIZE)),
            ],
            scratch_shapes=[
                pltpu.VMEM((span, rows), jnp.float32),
                pltpu.VMEM((span, HEAD_SIZE), jnp.float32),
                pltpu.VMEM((span, HEAD_SIZE), jnp.float32),
                pltpu.VMEM((rows, block), jnp.bfloat16),
            ],
        ),
        out_shape=[
            jax.ShapeDtypeStruct((rows, width), jnp.bfloat16),
            jax.ShapeDtypeStruct((2, reach * rows, HEAD_SIZE), jnp.bfloat16),
            jax.ShapeDtypeStruct((2, rows, HEAD_SIZE), jnp.float32),
        ],
        compiler_params=pltpu.CompilerParams(
            dimension_semantics=("arbitrary",), vmem_limit_bytes=VMEM_LIMIT
        ),
        name="attend",
    )(doc_lengths, *window, queries, grad_out)


def scatter_kernel(
    n_ctx, n_tp, reach, share, far_ref, own_ref, cos_ref, sin_ref, key_out, value_out,
    acc, landed, staged, pieces, send_sem, recv_sem, piece_send, piece_recv,
):
    rows = own_ref.shape[1]
    items = rows // n_tp
    me = lax.axis_index("ctx")
    at = lax.axis_index("tp")
    greet(
        [(me - s >= 0, (lax.rem(me - s + n_ctx, n_ctx), at)) for s in range(1, reach + 1)]
        + [(me + s < n_ctx, (lax.rem(me + s, n_ctx), at)) for s in range(1, reach + 1)]
        + [(at >= 0, (me, lax.rem(at + t, n_tp))) for t in range(1, n_tp)]
    )

    def copy(s):
        return pltpu.make_async_remote_copy(
            src_ref=far_ref.at[:, pl.ds((reach - s) * rows, rows), :],
            dst_ref=landed.at[s - 1],
            send_sem=send_sem.at[s - 1],
            recv_sem=recv_sem.at[s - 1],
            device_id=(lax.rem(me - s + n_ctx, n_ctx), at),
            device_id_type=MESH,
        )

    for s in range(reach, 0, -1):
        @pl.when(me - s >= 0)
        def _():
            copy(s).start()
    acc[...] = own_ref[...]
    for s in range(1, reach + 1):
        @pl.when(me + s < n_ctx)
        def _():
            copy(s).wait_recv()
            acc[...] += landed[s - 1].astype(jnp.float32)
    grad = acc[0]
    turned = grad * cos_ref[...] - pltpu.roll(grad, HALF, 1) * sin_ref[...]
    staged[0] = turned.astype(staged.dtype)
    staged[1] = acc[1].astype(staged.dtype)

    def piece(t):
        to = lax.rem(at + t, n_tp)
        return pltpu.make_async_remote_copy(
            src_ref=staged.at[:, pl.ds(pl.multiple_of(to * items, items), items), :],
            dst_ref=pieces.at[t],
            send_sem=piece_send.at[t - 1],
            recv_sem=piece_recv.at[t - 1],
            device_id=(me, to),
            device_id_type=MESH,
        )

    for t in range(1, n_tp):
        piece(t).start()
    pieces[0] = staged[:, pl.ds(pl.multiple_of(at * items, items), items), :]
    for t in range(1, n_tp):
        piece(t).wait_recv()
    for head in range(KV_HEAD_COUNT):
        cols = slice(head * HEAD_SIZE, (head + 1) * HEAD_SIZE)
        total = None
        for other in range(head * share, (head + 1) * share):
            got = pieces[lax.rem(at - other + n_tp, n_tp)]
            total = got if total is None else total + got
        key_out[:, cols] = total[0].astype(jnp.bfloat16)
        value_out[:, cols] = total[1].astype(jnp.bfloat16)
    for t in range(1, n_tp):
        piece(t).wait_send()
    for s in range(1, reach + 1):
        @pl.when(me - s >= 0)
        def _():
            copy(s).wait_send()


def scatter(far, own, cos_wide, sin_wide, n_ctx, n_tp, reach, share):
    rows = own.shape[1]
    items = rows // n_tp
    between = jnp.bfloat16 if share == 1 else jnp.float32
    vmem = pl.BlockSpec(memory_space=pltpu.VMEM)
    width = KV_HEAD_COUNT * HEAD_SIZE
    return pl.pallas_call(
        functools.partial(scatter_kernel, n_ctx, n_tp, reach, share),
        out_shape=[jax.ShapeDtypeStruct((items, width), jnp.bfloat16)] * 2,
        in_specs=[vmem] * 4,
        out_specs=[vmem] * 2,
        scratch_shapes=[
            pltpu.VMEM((2, rows, HEAD_SIZE), jnp.float32),
            pltpu.VMEM((reach, 2, rows, HEAD_SIZE), jnp.bfloat16),
            pltpu.VMEM((2, rows, HEAD_SIZE), between),
            pltpu.VMEM((n_tp, 2, items, HEAD_SIZE), between),
            pltpu.SemaphoreType.DMA((reach,)),
            pltpu.SemaphoreType.DMA((reach,)),
            pltpu.SemaphoreType.DMA((n_tp - 1,)),
            pltpu.SemaphoreType.DMA((n_tp - 1,)),
        ],
        compiler_params=pltpu.CompilerParams(
            collective_id=1, has_side_effects=True, vmem_limit_bytes=VMEM_LIMIT
        ),
        name="scatter_grads",
    )(far, own, cos_wide, sin_wide)


def local(queries, keys, values, grad_out, doc_lengths):
    rows = queries.shape[0]
    heads = queries.shape[1] // HEAD_SIZE
    n_ctx = lax.axis_size("ctx")
    n_tp = lax.axis_size("tp")
    share = max(1, QUERY_PER_KV // heads)
    reach = min(-(-MAXDOC // rows), n_ctx - 1)
    window = gather(keys, values, doc_lengths, heads, n_ctx, reach)
    cos_wide, sin_wide = window[3], window[4]
    grad_queries, far, near = attend(window, queries, grad_out, doc_lengths, reach)
    keys_gradient, values_gradient = scatter(
        far, near, cos_wide, sin_wide, n_ctx, n_tp, reach, share
    )
    return grad_queries, keys_gradient, values_gradient


def solution(mesh):
    return jax.shard_map(
        local,
        mesh=mesh,
        in_specs=(P("ctx", "tp"), P("ctx", None), P("ctx", None), P("ctx", "tp"), P()),
        out_specs=(P("ctx", "tp"), P(("ctx", "tp"), None), P(("ctx", "tp"), None)),
        check_vma=False,
    )
```

```python
import functools
import math

import jax
import jax.numpy as jnp
from jax import lax
from jax.experimental import pallas as pl
from jax.experimental.pallas import tpu as pltpu
from jax.sharding import PartitionSpec as P

KV_HEAD_COUNT = 4
HEAD_SIZE = 128
QUERY_PER_KV = 16
MAXDOC = 1024
NEG = -1e30
HALF = HEAD_SIZE // 2
SCALE = HEAD_SIZE ** (-0.5)
LOG2E = math.log2(math.e)
HEADS_PER_STEP = 4
VMEM_LIMIT = 60 << 20
MESH = pl.DeviceIdType.MESH


def greet(peers):
    barrier = pltpu.get_barrier_semaphore()
    count = 0
    for live, device in peers:
        @pl.when(live)
        def _():
            pl.semaphore_signal(barrier, inc=1, device_id=device, device_id_type=MESH)
        count = count + live.astype(jnp.int32)
    pl.semaphore_wait(barrier, count)


def doc_starts(lengths_ref, tok):
    start = jnp.int32(0)
    found = jnp.zeros_like(tok)
    for d in range(lengths_ref.shape[0]):
        found = jnp.where(tok >= start, start, found)
        start = start + lengths_ref[d]
    return found


def gather_kernel(
    n_ctx, reach, heads, lengths_ref, keys_ref, values_ref,
    rk_ref, v_ref, kt_ref, cos_ref, sin_ref, cos_t_ref, sin_t_ref,
    raw, cos_all, sin_all, send_sem, recv_sem, local_sem,
):
    rows = keys_ref.shape[0]
    me = lax.axis_index("ctx")
    at = lax.axis_index("tp")
    head = at * heads // QUERY_PER_KV
    cols = pl.ds(pl.multiple_of(head * HEAD_SIZE, HEAD_SIZE), HEAD_SIZE)
    here = pl.ds(reach * rows, rows)
    own_key = pltpu.make_async_copy(keys_ref.at[:, cols], raw.at[0, here, :], local_sem.at[0])
    own_value = pltpu.make_async_copy(values_ref.at[:, cols], raw.at[1, here, :], local_sem.at[1])
    own_key.start()
    own_value.start()
    greet(
        [(me + s < n_ctx, (lax.rem(me + s, n_ctx), at)) for s in range(1, reach + 1)]
        + [(me - s >= 0, (lax.rem(me - s + n_ctx, n_ctx), at)) for s in range(1, reach + 1)]
    )
    own_key.wait()
    own_value.wait()

    def copy(s):
        return pltpu.make_async_remote_copy(
            src_ref=raw.at[:, here, :],
            dst_ref=raw.at[:, pl.ds((reach - s) * rows, rows), :],
            send_sem=send_sem.at[s - 1],
            recv_sem=recv_sem.at[s - 1],
            device_id=(lax.rem(me + s, n_ctx), at),
            device_id_type=MESH,
        )

    for s in range(reach, 0, -1):
        @pl.when(me + s < n_ctx)
        def _():
            copy(s).start()

    index = lax.broadcasted_iota(jnp.int32, (HALF, HEAD_SIZE), 0).astype(jnp.float32)
    freq = jnp.exp2(index * (-2.0 / HEAD_SIZE * math.log2(500000.0)))[:, :1]
    for slot in range(reach, -1, -1):
        lanes = slice(slot * rows, (slot + 1) * rows)
        tok = lax.broadcasted_iota(jnp.int32, (1, rows), 1) + (me - reach + slot) * rows
        pos = (tok - doc_starts(lengths_ref, tok)).astype(jnp.float32)
        angle = pos * freq
        cos_all[:, lanes] = jnp.cos(angle)
        sin_all[:, lanes] = jnp.sin(angle)
    cos = cos_all[:, reach * rows :]
    sin = sin_all[:, reach * rows :]
    cos_t_ref[...] = cos
    sin_t_ref[...] = sin
    cos_ref[...] = jnp.concatenate([cos, cos], axis=0).T
    sin_ref[...] = jnp.concatenate([-sin, sin], axis=0).T

    def turn(slot):
        lanes = slice(slot * rows, (slot + 1) * rows)
        key = raw[0, lanes, :].astype(jnp.float32).T
        one, two = key[:HALF], key[HALF:]
        c, s = cos_all[:, lanes], sin_all[:, lanes]
        key = jnp.concatenate([one * c - two * s, two * c + one * s], axis=0)
        kt_ref[:, lanes] = key.astype(jnp.bfloat16)
        rk_ref[lanes, :] = key.T.astype(jnp.bfloat16)
        v_ref[lanes, :] = raw[1, lanes, :]

    turn(reach)
    for s in range(1, reach + 1):
        @pl.when(me - s >= 0)
        def _():
            copy(s).wait_recv()
            turn(reach - s)
    for s in range(1, reach + 1):
        @pl.when(me + s < n_ctx)
        def _():
            copy(s).wait_send()


def gather(keys, values, doc_lengths, heads, n_ctx, reach):
    rows = keys.shape[0]
    span = (reach + 1) * rows
    vmem = pl.BlockSpec(memory_space=pltpu.VMEM)
    hbm = pl.BlockSpec(memory_space=pltpu.HBM)
    return pl.pallas_call(
        functools.partial(gather_kernel, n_ctx, reach, heads),
        out_shape=[
            jax.ShapeDtypeStruct((span, HEAD_SIZE), jnp.bfloat16),
            jax.ShapeDtypeStruct((span, HEAD_SIZE), jnp.bfloat16),
            jax.ShapeDtypeStruct((HEAD_SIZE, span), jnp.bfloat16),
            jax.ShapeDtypeStruct((rows, HEAD_SIZE), jnp.float32),
            jax.ShapeDtypeStruct((rows, HEAD_SIZE), jnp.float32),
            jax.ShapeDtypeStruct((HALF, rows), jnp.float32),
            jax.ShapeDtypeStruct((HALF, rows), jnp.float32),
        ],
        in_specs=[pl.BlockSpec(memory_space=pltpu.SMEM), hbm, hbm],
        out_specs=[vmem] * 7,
        scratch_shapes=[
            pltpu.VMEM((2, span, HEAD_SIZE), jnp.bfloat16),
            pltpu.VMEM((HALF, span), jnp.float32),
            pltpu.VMEM((HALF, span), jnp.float32),
            pltpu.SemaphoreType.DMA((reach,)),
            pltpu.SemaphoreType.DMA((reach,)),
            pltpu.SemaphoreType.DMA((2,)),
        ],
        compiler_params=pltpu.CompilerParams(
            collective_id=0, has_side_effects=True, vmem_limit_bytes=VMEM_LIMIT
        ),
        name="gather_kv",
    )(doc_lengths, keys, values)


def attend_kernel(
    reach, rows, lengths_ref, rk_ref, v_ref, kt_ref, cos_ref, sin_ref, cos_t_ref, sin_t_ref,
    q_ref, g_ref, dq_ref, far_ref, own_ref, bias, dk, dv, rots,
):
    step = pl.program_id(0)
    span = (reach + 1) * rows
    half = rows // 2
    first = lax.axis_index("ctx") * rows

    @pl.when(step == 0)
    def _():
        query = lax.broadcasted_iota(jnp.int32, (1, rows), 1) + reach * rows
        start = doc_starts(lengths_ref, query + (first - reach * rows)) - (first - reach * rows)
        key = lax.broadcasted_iota(jnp.int32, (span, rows), 0)
        bias[...] = jnp.where((key >= start) & (key <= query), 0.0, NEG)
        dk[...] = jnp.zeros_like(dk)
        dv[...] = jnp.zeros_like(dv)

    nt = (((1,), (1,)), ((), ()))
    for i in range(HEADS_PER_STEP):
        cols = slice(i * HEAD_SIZE, (i + 1) * HEAD_SIZE)
        raw = q_ref[:, cols].astype(jnp.float32)
        rot = raw * cos_ref[...] + pltpu.roll(raw, HALF, 1) * sin_ref[...]
        rots[:, cols] = rot.astype(jnp.bfloat16)

    def pick(ref, side, pair):
        return jnp.concatenate(
            [
                ref[side * half : (side + 1) * half, i * HEAD_SIZE : (i + 1) * HEAD_SIZE]
                for i in (2 * pair, 2 * pair + 1)
            ],
            axis=0,
        )

    def twice(x):
        return jnp.concatenate([x, x], axis=1)

    def work(side, count):
        end = span - half + side * half
        base = end - count * half
        keys = rk_ref[base:end, :]
        values = v_ref[base:end, :]
        lanes = slice(side * half, (side + 1) * half)
        mask = twice(bias[base:end, lanes])
        c, s = twice(cos_t_ref[:, lanes]), twice(sin_t_ref[:, lanes])
        probs, grads, dscores, queries = [], [], [], []
        for pair in range(HEADS_PER_STEP // 2):
            rot = pick(rots, side, pair)
            grad = pick(g_ref, side, pair)
            score = lax.dot_general(keys, rot, nt, preferred_element_type=jnp.float32)
            score = score * (SCALE * LOG2E) + mask
            top = jnp.max(score, axis=0, keepdims=True)
            expo = jnp.exp2(score - top)
            total = jnp.sum(expo, axis=0, keepdims=True)
            dprod = lax.dot_general(values, grad, nt, preferred_element_type=jnp.float32)
            weighted = jnp.sum(expo * dprod, axis=0, keepdims=True)
            inv = 1.0 / total
            delta = weighted * inv
            probs.append(expo.astype(jnp.bfloat16))
            dscore = (expo * (dprod - delta)).astype(jnp.bfloat16)
            dscores.append(dscore)
            spread = jnp.broadcast_to(inv, (HEAD_SIZE, 2 * half)).T
            grads.append((grad.astype(jnp.float32) * spread).astype(jnp.bfloat16))
            queries.append((rot.astype(jnp.float32) * (spread * SCALE)).astype(jnp.bfloat16))
            dq = jnp.dot(kt_ref[:, base:end], dscore, preferred_element_type=jnp.float32)
            dq = dq * (inv * SCALE)
            one, two = dq[:HALF], dq[HALF:]
            turned = jnp.concatenate([one * c + two * s, two * c - one * s], axis=0)
            turned = turned.astype(jnp.bfloat16).T
            for i in range(2):
                at = (2 * pair + i) * HEAD_SIZE
                dq_ref[lanes, at : at + HEAD_SIZE] = turned[i * half : (i + 1) * half, :]
        dv[base:end, :] += jnp.dot(
            jnp.concatenate(probs, axis=1), jnp.concatenate(grads, axis=0),
            preferred_element_type=jnp.float32,
        )
        dk[base:end, :] += jnp.dot(
            jnp.concatenate(dscores, axis=1), jnp.concatenate(queries, axis=0),
            preferred_element_type=jnp.float32,
        )

    for side in range(2):
        tok = first + side * half
        low = doc_starts(lengths_ref, tok) - (first - reach * rows)
        most = 2 * reach + 1 + side
        tiles = most - low // half
        for count in range(1, most + 1):
            @pl.when(tiles == count)
            def _():
                work(side, count)

    @pl.when(step == pl.num_programs(0) - 1)
    def _():
        far_ref[0] = dk[: reach * rows, :].astype(jnp.bfloat16)
        far_ref[1] = dv[: reach * rows, :].astype(jnp.bfloat16)
        own_ref[0] = dk[reach * rows :, :]
        own_ref[1] = dv[reach * rows :, :]


def attend(window, queries, grad_out, doc_lengths, reach):
    rows, width = queries.shape
    span = (reach + 1) * rows
    block = HEADS_PER_STEP * HEAD_SIZE

    def whole(shape):
        return pl.BlockSpec(shape, lambda i, low: (0,) * len(shape))

    by_head = pl.BlockSpec((rows, block), lambda i, low: (0, i))
    return pl.pallas_call(
        functools.partial(attend_kernel, reach, rows),
        grid_spec=pltpu.PrefetchScalarGridSpec(
            num_scalar_prefetch=1,
            grid=(width // block,),
            in_specs=[whole(x.shape) for x in window] + [by_head, by_head],
            out_specs=[
                by_head, whole((2, reach * rows, HEAD_SIZE)), whole((2, rows, HEAD_SIZE)),
            ],
            scratch_shapes=[
                pltpu.VMEM((span, rows), jnp.float32),
                pltpu.VMEM((span, HEAD_SIZE), jnp.float32),
                pltpu.VMEM((span, HEAD_SIZE), jnp.float32),
                pltpu.VMEM((rows, block), jnp.bfloat16),
            ],
        ),
        out_shape=[
            jax.ShapeDtypeStruct((rows, width), jnp.bfloat16),
            jax.ShapeDtypeStruct((2, reach * rows, HEAD_SIZE), jnp.bfloat16),
            jax.ShapeDtypeStruct((2, rows, HEAD_SIZE), jnp.float32),
        ],
        compiler_params=pltpu.CompilerParams(
            dimension_semantics=("arbitrary",), vmem_limit_bytes=VMEM_LIMIT
        ),
        name="attend",
    )(doc_lengths, *window, queries, grad_out)


def scatter_kernel(
    n_ctx, n_tp, reach, share, far_ref, own_ref, cos_ref, sin_ref, key_out, value_out,
    acc, landed, staged, pieces, send_sem, recv_sem, piece_send, piece_recv,
):
    rows = own_ref.shape[1]
    items = rows // n_tp
    me = lax.axis_index("ctx")
    at = lax.axis_index("tp")
    greet(
        [(me - s >= 0, (lax.rem(me - s + n_ctx, n_ctx), at)) for s in range(1, reach + 1)]
        + [(me + s < n_ctx, (lax.rem(me + s, n_ctx), at)) for s in range(1, reach + 1)]
        + [(at >= 0, (me, lax.rem(at + t, n_tp))) for t in range(1, n_tp)]
    )

    def copy(s):
        return pltpu.make_async_remote_copy(
            src_ref=far_ref.at[:, pl.ds((reach - s) * rows, rows), :],
            dst_ref=landed.at[s - 1],
            send_sem=send_sem.at[s - 1],
            recv_sem=recv_sem.at[s - 1],
            device_id=(lax.rem(me - s + n_ctx, n_ctx), at),
            device_id_type=MESH,
        )

    for s in range(reach, 0, -1):
        @pl.when(me - s >= 0)
        def _():
            copy(s).start()
    acc[...] = own_ref[...]
    for s in range(1, reach + 1):
        @pl.when(me + s < n_ctx)
        def _():
            copy(s).wait_recv()
            acc[...] += landed[s - 1].astype(jnp.float32)
    grad = acc[0]
    turned = grad * cos_ref[...] - pltpu.roll(grad, HALF, 1) * sin_ref[...]
    staged[0] = turned.astype(staged.dtype)
    staged[1] = acc[1].astype(staged.dtype)

    def piece(t):
        to = lax.rem(at + t, n_tp)
        return pltpu.make_async_remote_copy(
            src_ref=staged.at[:, pl.ds(pl.multiple_of(to * items, items), items), :],
            dst_ref=pieces.at[t],
            send_sem=piece_send.at[t - 1],
            recv_sem=piece_recv.at[t - 1],
            device_id=(me, to),
            device_id_type=MESH,
        )

    for t in range(1, n_tp):
        piece(t).start()
    pieces[0] = staged[:, pl.ds(pl.multiple_of(at * items, items), items), :]
    for t in range(1, n_tp):
        piece(t).wait_recv()
    for head in range(KV_HEAD_COUNT):
        cols = slice(head * HEAD_SIZE, (head + 1) * HEAD_SIZE)
        total = None
        for other in range(head * share, (head + 1) * share):
            got = pieces[lax.rem(at - other + n_tp, n_tp)]
            total = got if total is None else total + got
        key_out[:, cols] = total[0].astype(jnp.bfloat16)
        value_out[:, cols] = total[1].astype(jnp.bfloat16)
    for t in range(1, n_tp):
        piece(t).wait_send()
    for s in range(1, reach + 1):
        @pl.when(me - s >= 0)
        def _():
            copy(s).wait_send()


def scatter(far, own, cos_wide, sin_wide, n_ctx, n_tp, reach, share):
    rows = own.shape[1]
    items = rows // n_tp
    between = jnp.bfloat16 if share == 1 else jnp.float32
    vmem = pl.BlockSpec(memory_space=pltpu.VMEM)
    width = KV_HEAD_COUNT * HEAD_SIZE
    return pl.pallas_call(
        functools.partial(scatter_kernel, n_ctx, n_tp, reach, share),
        out_shape=[jax.ShapeDtypeStruct((items, width), jnp.bfloat16)] * 2,
        in_specs=[vmem] * 4,
        out_specs=[vmem] * 2,
        scratch_shapes=[
            pltpu.VMEM((2, rows, HEAD_SIZE), jnp.float32),
            pltpu.VMEM((reach, 2, rows, HEAD_SIZE), jnp.bfloat16),
            pltpu.VMEM((2, rows, HEAD_SIZE), between),
            pltpu.VMEM((n_tp, 2, items, HEAD_SIZE), between),
            pltpu.SemaphoreType.DMA((reach,)),
            pltpu.SemaphoreType.DMA((reach,)),
            pltpu.SemaphoreType.DMA((n_tp - 1,)),
            pltpu.SemaphoreType.DMA((n_tp - 1,)),
        ],
        compiler_params=pltpu.CompilerParams(
            collective_id=1, has_side_effects=True, vmem_limit_bytes=VMEM_LIMIT
        ),
        name="scatter_grads",
    )(far, own, cos_wide, sin_wide)


def local(queries, keys, values, grad_out, doc_lengths):
    rows = queries.shape[0]
    heads = queries.shape[1] // HEAD_SIZE
    n_ctx = lax.axis_size("ctx")
    n_tp = lax.axis_size("tp")
    share = max(1, QUERY_PER_KV // heads)
    reach = min(-(-MAXDOC // rows), n_ctx - 1)
    window = gather(keys, values, doc_lengths, heads, n_ctx, reach)
    cos_wide, sin_wide = window[3], window[4]
    grad_queries, far, near = attend(window, queries, grad_out, doc_lengths, reach)
    keys_gradient, values_gradient = scatter(
        far, near, cos_wide, sin_wide, n_ctx, n_tp, reach, share
    )
    return grad_queries, keys_gradient, values_gradient


def solution(mesh):
    return jax.shard_map(
        local,
        mesh=mesh,
        in_specs=(P("ctx", "tp"), P("ctx", None), P("ctx", None), P("ctx", "tp"), P()),
        out_specs=(P("ctx", "tp"), P(("ctx", "tp"), None), P(("ctx", "tp"), None)),
        check_vma=False,
    )
```
